768 devices in a mesh: blk: 128 (over z_hi, x, y), col: 6 (over z_lo, core).
Axes of the slice: x: 4, y: 8, z: 12 (z_hi: 4, z_lo: 3; z = z_hi * 3 + z_lo), core: 2. Of those that a mesh axis runs over, the one named last changes fastest.
Arguments:
- psi: bfloat16 [256, 384, 384], P('blk', 'col')
- dims: int32 [256], P('blk'), may hold values from 192 to 384, as said below
- pattern: int32 [256, 5], P('blk'), may hold values 0 or 1
- left_env: bfloat16 [256, 12, 384, 384], P('blk', 'col')
- right_env: bfloat16 [12, 384, 384], P('col')
Outputs:
- sigma_first: float32 [256, 384, 384], P('blk', 'col')
- sigma_second: float32 [256, 384, 384], P('blk', 'col')
The draws below stay inside these ranges and needn't reach their ends.
Inputs may be any that keep to these rules, and one draw needn't show every extreme that they name: dims[s] lies between 192 and 384.
All inputs are finite; a program needn't handle non-finite values. No bound on the sum of `pattern` on one device may be relied on, other than what follows from the above.
Results may differ from the reference program's by a relative error of at most 0.022.
Values may be sent and summed in bfloat16 or wider, within the bound.
No kernel may reach another device: no remote copies, remote signals or barrier semaphores. Data moves between devices by JAX's collectives and lax.ppermute only.
A program may use at most 32 MiB of HBM per device.

```python
import jax
import jax.numpy as jnp
from jax import lax

BS = 384
W_COL = 2
NOFF = 5
SECTORS = 256
W = 12
N_COL = 6


def row_signs(key):
    bits = jax.random.randint(jax.random.fold_in(key, 5), (SECTORS, BS), 0, 2)
    return (2 * bits - 1).astype(jnp.float32)


def draw_psi(key, part):
    signs = row_signs(key)
    key = jax.random.fold_in(key, 11)
    first = jax.random.fold_in(key, 0)
    sector = jnp.arange(SECTORS, dtype=jnp.float32)
    rise = jnp.exp(0.5 * jnp.log(3.0) * sector / max(SECTORS - 1, 1))
    tilt = jnp.where(signs > 0.0, 2.0, 0.5)[:, :, None]
    base = jax.random.normal(first, (SECTORS, BS, BS), jnp.float32)
    return (base * rise[:, None, None] * tilt).astype(jnp.bfloat16)


def draw_dims(key, part):
    key = jax.random.fold_in(key, 23)
    first, second, third = jax.random.split(key, 3)
    values = jax.random.randint(first, (SECTORS,), BS // 2, BS + 1)
    top_at = jax.random.randint(second, (), 0, SECTORS)
    step = jax.random.randint(third, (), 1, SECTORS)
    low_at = (top_at + step) % SECTORS
    values = values.at[top_at].set(BS)
    values = values.at[low_at].set(BS // 2)
    return values.astype(jnp.int32)


def env_noise(key, shape):
    values = jax.random.normal(key, shape, jnp.float32)
    return values / jnp.sqrt(jnp.float32(BS))


def draw_left_env(key, part):
    signs = row_signs(key)
    key = jax.random.fold_in(key, 37)
    noise = env_noise(key, (SECTORS, W, BS, BS))
    sector = jnp.arange(SECTORS, dtype=jnp.float32) / max(SECTORS - 1, 1)
    level = -1.0 + 3.0 * sector
    shift = jnp.float32(W) ** 0.25
    entries = shift * (level[:, None] + 0.5 * signs)
    diag = entries[:, :, None] * jnp.eye(BS, dtype=jnp.float32)[None, :, :]
    noise = noise.at[:, 0].add(diag)
    return noise.astype(jnp.bfloat16)


def draw_right_env(key, part):
    key = jax.random.fold_in(key, 41)
    noise = env_noise(key, (W, BS, BS))
    shift = jnp.float32(W) ** 0.25
    noise = noise.at[0].add(shift * jnp.eye(BS, dtype=jnp.float32))
    return noise.astype(jnp.bfloat16)


def with_ends(array, own_key, smallest, high):
    longest = array.shape.index(max(array.shape))
    spots = []
    for shift in (0, 1):
        where = [jax.random.randint(jax.random.fold_in(own_key, axis), (), 0, length) for axis, length in enumerate(array.shape)]
        where[longest] = (where[longest] + shift) % array.shape[longest]
        spots.append(tuple(where))
    return array.at[spots[0]].set(smallest).at[spots[1]].set(high)


def setup_inputs(seed: int = 0) -> dict:
    streams_of = jax.random.split(jax.random.key(seed), 6)
    psi = draw_psi(jax.random.fold_in(streams_of[5], 71), 0)
    dims = draw_dims(jax.random.fold_in(streams_of[5], 71), 0)
    pattern = with_ends((jax.random.randint(streams_of[2], (SECTORS, NOFF), 0, 4) < 3).astype(jnp.int32), jax.random.fold_in(streams_of[2], 1), 0, 1)
    left_env = draw_left_env(jax.random.fold_in(streams_of[5], 71), 0)
    right_env = draw_right_env(jax.random.fold_in(streams_of[5], 71), 0)
    return dict(psi=psi, dims=dims, pattern=pattern, left_env=left_env, right_env=right_env)


def block_mask(dims):
    index = jnp.arange(BS)
    inside = index[None, :] < dims[:, None]
    return inside[:, :, None] & inside[:, None, :]

def combine_blocks(vector, pattern):
    padded = jnp.pad(vector.astype(jnp.float32), ((2, 2), (0, 0), (0, 0)))
    coeff = pattern.astype(jnp.float32)
    total = jnp.zeros(vector.shape, jnp.float32)
    for offset in range(NOFF):
        total = total + coeff[:, offset, None, None] * padded[offset:offset + SECTORS]
    return total.astype(jnp.bfloat16)

def apply_hamiltonian(vector, pattern, left_env, right_env, mask):
    combined = combine_blocks(vector, pattern)
    right_groups = right_env.astype(jnp.float32).reshape(N_COL, W_COL, BS, BS)

    def one_sector(inputs):
        left_block, z_block = inputs
        temp = jnp.einsum('wab,bc->wac', left_block.astype(jnp.float32), z_block.astype(jnp.float32)).astype(jnp.bfloat16)
        temp = temp.astype(jnp.float32).reshape(N_COL, W_COL, BS, BS)
        parts = jnp.einsum('gwac,gwdc->gad', temp, right_groups)
        parts = lax.optimization_barrier(parts.astype(jnp.bfloat16))
        return lax.optimization_barrier(jnp.sum(parts.astype(jnp.float32), axis=0))
    summed = lax.map(one_sector, (left_env, combined))
    return jnp.where(mask, summed / jnp.sqrt(jnp.float32(W)), jnp.float32(0.0))

def reference(psi, dims, pattern, left_env, right_env):
    mask = block_mask(dims)
    psi_m = jnp.where(mask, psi, jnp.zeros_like(psi))
    sigma_first = apply_hamiltonian(psi_m, pattern, left_env, right_env, mask)
    psi_float = psi_m.astype(jnp.float32)
    theta = jnp.sum(psi_float * sigma_first) / jnp.sum(psi_float * psi_float)
    resid = (sigma_first - theta * psi_float).astype(jnp.bfloat16)
    sigma_second = apply_hamiltonian(resid, pattern, left_env, right_env, mask)
    return (sigma_first, sigma_second)
```

```python
import jax
import jax.numpy as jnp
from jax import lax
from jax.sharding import PartitionSpec as P

CORES = 2


def combine_rows(vector, pattern):
    count = lax.axis_size("blk")
    forward = [(i, i + 1) for i in range(count - 1)]
    backward = [(target, source) for source, target in forward]
    low = lax.ppermute(vector, "blk", forward)
    high = lax.ppermute(vector, "blk", backward)
    padded = jnp.concatenate([low, vector, high], axis=0).astype(jnp.float32)
    coeff = pattern.astype(jnp.float32)
    sectors = vector.shape[0]
    total = jnp.zeros(vector.shape, jnp.float32)
    for offset in range(pattern.shape[1]):
        total = total + coeff[:, offset, None, None] * padded[offset : offset + sectors]
    return total.astype(jnp.bfloat16)


def exchange_sum(values, axis):
    copies = jnp.broadcast_to(values[None, :, None], (lax.axis_size(axis), values.shape[0], 128))
    return jnp.sum(lax.all_to_all(copies, axis, 0, 0, tiled=True)[:, :, 0], axis=0)


def apply_hamiltonian(vector, pattern, envs, mask, scale):
    sectors, rows, width = vector.shape
    count = lax.axis_size("col")
    rows_of_z = combine_rows(vector, pattern)
    outgoing = jnp.tile(rows_of_z, (count // CORES, 1, 1))
    combined = lax.all_to_all(outgoing, "col", 0, 0, tiled=True).reshape(count * rows, width)
    part = jnp.zeros((count * rows, width), jnp.float32)
    for left, right in envs:
        temp = jnp.einsum("wab,bc->wac", left, combined, preferred_element_type=jnp.float32)
        part = part + jnp.einsum(
            "wac,wdc->ad", temp.astype(jnp.bfloat16), right, preferred_element_type=jnp.float32
        )
    part = part.astype(jnp.bfloat16).reshape(count, rows, width)
    mine = lax.all_to_all(part, "col", 0, 0, tiled=True).astype(jnp.float32)
    summed = jnp.sum(mine.reshape(count // CORES, sectors, rows, width), axis=0)
    return jnp.where(mask, summed * scale, jnp.float32(0.0))


def body(psi, dims, pattern, left_env, right_env):
    rows = psi.shape[1]
    width = psi.shape[2]
    count = lax.axis_size("col")
    core = lax.rem(lax.axis_index("col"), CORES)
    swap = [(i, i ^ 1) for i in range(count)]
    left_mine = lax.dynamic_index_in_dim(left_env, core, 0, keepdims=False)
    left_sent = lax.dynamic_index_in_dim(left_env, 1 - core, 0, keepdims=False)
    row_ids = lax.axis_index("col") * rows + jnp.arange(rows, dtype=jnp.int32)
    col_ids = jnp.arange(width, dtype=jnp.int32)
    mask = (row_ids[None, :, None] < dims[:, None, None]) & (
        col_ids[None, None, :] < dims[:, None, None]
    )
    psi_m = jnp.where(mask, psi, jnp.zeros_like(psi))
    envs = (
        (left_mine, right_env),
        (lax.ppermute(left_sent, "col", swap), lax.ppermute(right_env, "col", swap)),
    )
    scale = 1.0 / jnp.sqrt(jnp.float32(right_env.shape[0] * count))
    sigma_first = apply_hamiltonian(psi_m, pattern, envs, mask, scale)
    psi_float = psi_m.astype(jnp.float32)
    products = jnp.stack([jnp.sum(psi_float * sigma_first), jnp.sum(psi_float * psi_float)])
    sums = exchange_sum(exchange_sum(products, "blk"), "col")
    theta = sums[0] / sums[1]
    applied = apply_hamiltonian(sigma_first.astype(jnp.bfloat16), pattern, envs, mask, scale)
    return (sigma_first, applied - theta * sigma_first)


def solution(mesh):
    return jax.shard_map(
        body,
        mesh=mesh,
        in_specs=(
            P("blk", "col", None),
            P("blk"),
            P("blk", None),
            P("blk", "col", None, None),
            P("col", None, None),
        ),
        out_specs=(P("blk", "col", None), P("blk", "col", None)),
        check_vma=False,
    )
```

```python
import jax
import jax.numpy as jnp
from jax import lax
from jax.sharding import Mesh, PartitionSpec as P

CORES = 2
LANES = 128
SPLIT = {"z_hi": 4, "x": 4, "y": 8, "z_lo": 3, "core": 2}
BLK = ("z_hi", "x", "y")
COL = ("z_lo", "core")
NEAR = ("x", "y")
FAR = ("z_hi", "z_lo", "core")
F32 = jnp.float32
BF16 = jnp.bfloat16


def exchange(blocks, axes):
    return lax.all_to_all(blocks, axes, 0, 0, tiled=True)


def masked(value, dims):
    _, rows, width = value.shape
    dims = lax.optimization_barrier(dims)[:, None, None]
    row = lax.broadcasted_iota(jnp.int32, value.shape, 1) + lax.axis_index(COL) * rows
    column = lax.broadcasted_iota(jnp.int32, value.shape, 2)
    return jnp.where((row < dims) & (column < dims), value, jnp.zeros_like(value))


def combine(vector, coeff):
    count = lax.axis_size(BLK)
    forward = [(i, i + 1) for i in range(count - 1)]
    backward = [(target, source) for source, target in forward]
    low = lax.ppermute(vector, BLK, forward)
    high = lax.ppermute(vector, BLK, backward)
    padded = jnp.concatenate([low, vector, high], axis=0).astype(F32)
    sectors, rows, width = vector.shape
    total = jnp.zeros(coeff.shape[:2] + (rows, width), F32)
    for offset in range(coeff.shape[2]):
        total = total + coeff[:, :, offset, None, None] * padded[None, offset : offset + sectors]
    return total.astype(BF16).reshape(-1, rows, width)


def product(z, left, right):
    count, rows, width = z.shape
    z = z.reshape(count * rows, width)
    temp = jnp.einsum("wab,bc->wac", left, z, preferred_element_type=F32).astype(BF16)
    part = jnp.einsum("wac,wdc->ad", temp, right, preferred_element_type=F32)
    return part.astype(BF16).reshape(count, rows, width)


def reduced(parts, sectors, scale):
    count, rows, width = parts.shape
    parts = parts.astype(F32).reshape(count // sectors, sectors, rows, width)
    return jnp.sum(parts, axis=0) * scale


def gathered(values, axes):
    return exchange(jnp.broadcast_to(values[None, None, :], (lax.axis_size(axes), 1, LANES)), axes)


def body(psi, dims, pattern, left_env, right_env):
    sectors = psi.shape[0]
    count = lax.axis_size(COL)
    core = lax.axis_index("core")
    swap = [(0, 1), (1, 0)]
    scale = 1.0 / jnp.sqrt(F32(right_env.shape[0] * count))
    coeff = jnp.broadcast_to(pattern.astype(F32)[None], (count // CORES,) + pattern.shape)
    coeff = lax.optimization_barrier(coeff)

    psi_m = masked(psi, dims)
    outgoing = combine(psi_m, coeff)
    left_mine = lax.dynamic_index_in_dim(left_env, core, 0, keepdims=False)
    left_sent = lax.dynamic_index_in_dim(left_env, 1 - core, 0, keepdims=False)
    left = jnp.concatenate([left_mine, lax.ppermute(left_sent, "core", swap)], axis=0)
    right = jnp.concatenate([right_env, lax.ppermute(right_env, "core", swap)], axis=0)
    left, right = lax.optimization_barrier((left, right))
    parts = exchange(product(exchange(outgoing, COL), left, right), COL)
    sigma = masked(reduced(parts, sectors, scale), dims)
    vector = psi_m.astype(F32)
    products = jnp.where(
        jnp.arange(LANES) < LANES // 2, jnp.sum(vector * sigma), jnp.sum(vector * vector)
    )
    sums = jnp.sum(gathered(products, NEAR), axis=(0, 1))
    z = exchange(combine(sigma.astype(BF16), coeff), COL)
    z, sums = lax.optimization_barrier((z, sums))
    sums = jnp.sum(gathered(sums, FAR), axis=(0, 1))
    parts = exchange(product(z, left, right), COL)
    theta = sums[0] / sums[LANES // 2]
    second = masked(reduced(parts, sectors, scale), dims) - theta * sigma
    return (sigma, second)


def solution(mesh):
    split = Mesh(mesh.devices.reshape(tuple(SPLIT.values())), tuple(SPLIT))
    return jax.shard_map(
        body,
        mesh=split,
        in_specs=(
            P(BLK, COL, None),
            P(BLK),
            P(BLK, None),
            P(BLK, COL, None, None),
            P(COL, None, None),
        ),
        out_specs=(P(BLK, COL, None), P(BLK, COL, None)),
        check_vma=False,
    )
```

```python
import jax
import jax.numpy as jnp
from jax import lax
from jax.sharding import Mesh, PartitionSpec as P

CORES = 2
LANES = 128
SPLIT = {"z_hi": 4, "x": 4, "y": 8, "z_lo": 3, "core": 2}
BLK = ("z_hi", "x", "y")
COL = ("z_lo", "core")
NEAR = ("x", "y", "core")
F32 = jnp.float32
BF16 = jnp.bfloat16


def exchange(blocks, axes):
    return lax.all_to_all(blocks, axes, 0, 0, tiled=True)


def masked(value, dims):
    _, rows, width = value.shape
    dims = lax.optimization_barrier(dims)[:, None, None]
    row = lax.broadcasted_iota(jnp.int32, value.shape, 1) + lax.axis_index(COL) * rows
    column = lax.broadcasted_iota(jnp.int32, value.shape, 2)
    return jnp.where((row < dims) & (column < dims), value, jnp.zeros_like(value))


def combine(vector, coeff):
    count = lax.axis_size(BLK)
    near = [(i, i ^ 1) for i in range(count)]
    across = [(i, i + 1 if i % 2 else i - 1) for i in range(1, count - 1)]
    other = lax.ppermute(vector, BLK, across)
    partner = lax.ppermute(vector, BLK, near)
    odd = lax.rem(lax.axis_index(BLK), 2) == 1
    low, high = jnp.where(odd, partner, other), jnp.where(odd, other, partner)
    padded = jnp.concatenate([low, vector, high], axis=0).astype(F32)
    sectors, rows, width = vector.shape
    total = jnp.zeros(coeff.shape[:2] + (rows, width), F32)
    for offset in range(coeff.shape[2]):
        total = total + coeff[:, :, offset, None, None] * padded[None, offset : offset + sectors]
    return total.astype(BF16).reshape(-1, rows, width)


def product(z, left, right):
    count, rows, width = z.shape
    z = z.reshape(count * rows, width)
    temp = jnp.einsum("wab,bc->wac", left, z, preferred_element_type=F32).astype(BF16)
    part = jnp.einsum("wac,wdc->ad", temp, right, preferred_element_type=F32)
    return part.astype(BF16).reshape(count, rows, width)


def reduced(parts, sectors, scale):
    count, rows, width = parts.shape
    parts = parts.astype(F32).reshape(count // sectors, sectors, rows, width)
    return jnp.sum(parts, axis=0) * scale


def sum_by_exchange(values, axes):
    copies = jnp.broadcast_to(values[None], (lax.axis_size(axes), 1, LANES))
    return jnp.sum(exchange(copies, axes), axis=0)


def sum_by_permutes(values, axis, distances):
    count = lax.axis_size(axis)
    total = values
    for distance in distances:
        total = total + lax.ppermute(values, axis, [(i, (i + distance) % count) for i in range(count)])
    return total


def body(psi, dims, pattern, left_env, right_env):
    sectors = psi.shape[0]
    count = lax.axis_size(COL)
    core = lax.axis_index("core")
    swap = [(0, 1), (1, 0)]
    scale = 1.0 / jnp.sqrt(F32(right_env.shape[0] * count))
    coeff = jnp.broadcast_to(pattern.astype(F32)[None], (count // CORES,) + pattern.shape)
    coeff = lax.optimization_barrier(coeff)

    psi_m = masked(psi, dims)
    outgoing = combine(psi_m, coeff)
    left_mine = lax.dynamic_index_in_dim(left_env, core, 0, keepdims=False)
    left_sent = lax.dynamic_index_in_dim(left_env, 1 - core, 0, keepdims=False)
    left = jnp.concatenate([left_mine, lax.ppermute(left_sent, "core", swap)], axis=0)
    right = jnp.concatenate([right_env, lax.ppermute(right_env, "core", swap)], axis=0)
    left, right = lax.optimization_barrier((left, right))
    parts = exchange(product(exchange(outgoing, COL), left, right), COL)
    sigma = masked(reduced(parts, sectors, scale), dims)
    vector = psi_m.astype(F32)
    lane = lax.broadcasted_iota(jnp.int32, (1, LANES), 1)
    products = jnp.where(lane < LANES // 2, jnp.sum(vector * sigma), jnp.sum(vector * vector))
    outgoing = combine(sigma.astype(BF16), coeff)
    sums = sum_by_exchange(products, NEAR)
    outgoing, sums = lax.optimization_barrier((outgoing, sums))
    sums = sum_by_permutes(sums, "z_hi", (2,))
    part = product(exchange(outgoing, COL), left, right)
    part, sums = lax.optimization_barrier((part, sums))
    sums = sum_by_permutes(sums, "z_lo", (1, 2))
    sums = sum_by_permutes(sums, "z_hi", (1,))
    parts = exchange(part, COL)
    theta = sums[0, 0] / sums[0, LANES // 2]
    second = masked(reduced(parts, sectors, scale), dims) - theta * sigma
    return (sigma, second)


def solution(mesh):
    split = Mesh(mesh.devices.reshape(tuple(SPLIT.values())), tuple(SPLIT))
    return jax.shard_map(
        body,
        mesh=split,
        in_specs=(
            P(BLK, COL, None),
            P(BLK),
            P(BLK, None),
            P(BLK, COL, None, None),
            P(COL, None, None),
        ),
        out_specs=(P(BLK, COL, None), P(BLK, COL, None)),
        check_vma=False,
    )
```

```python
import jax
import jax.numpy as jnp
from jax import lax
from jax.sharding import Mesh, PartitionSpec as P

CORES = 2
LANES = 128
SPLIT = {"z_hi": 4, "x": 4, "y": 8, "z_lo": 3, "core": 2}
BLK = ("z_hi", "x", "y")
COL = ("z_lo", "core")
NEAR = ("x", "y", "core")
F32 = jnp.float32
BF16 = jnp.bfloat16


def exchange(blocks, axes):
    return lax.all_to_all(blocks, axes, 0, 0, tiled=True)


def masked(value, dims):
    _, rows, width = value.shape
    dims = lax.optimization_barrier(dims)[:, None, None]
    row = lax.broadcasted_iota(jnp.int32, value.shape, 1) + lax.axis_index(COL) * rows
    column = lax.broadcasted_iota(jnp.int32, value.shape, 2)
    return jnp.where((row < dims) & (column < dims), value, jnp.zeros_like(value))


def combine(vector, coeff):
    count = lax.axis_size(BLK)
    near = [(i, i ^ 1) for i in range(count)]
    across = [(i, i + 1 if i % 2 else i - 1) for i in range(1, count - 1)]
    other = lax.ppermute(vector, BLK, across)
    partner = lax.ppermute(vector, BLK, near)
    odd = lax.rem(lax.axis_index(BLK), 2) == 1
    low, high = jnp.where(odd, partner, other), jnp.where(odd, other, partner)
    padded = jnp.concatenate([low, vector, high], axis=0).astype(F32)
    sectors, rows, width = vector.shape
    total = jnp.zeros(coeff.shape[:2] + (rows, width), F32)
    for offset in range(coeff.shape[2]):
        total = total + coeff[:, :, offset, None, None] * padded[None, offset : offset + sectors]
    return total.astype(BF16).reshape(-1, rows, width)


def product(z, left, right):
    count, rows, width = z.shape
    z = z.reshape(count * rows, width)
    temp = jnp.einsum("wab,bc->wac", left, z, preferred_element_type=F32).astype(BF16)
    part = jnp.einsum("wac,wdc->ad", temp, right, preferred_element_type=F32)
    return part.astype(BF16).reshape(count, rows, width)


def reduced(parts, sectors, scale):
    count, rows, width = parts.shape
    parts = parts.astype(F32).reshape(count // sectors, sectors, rows, width)
    return jnp.sum(parts, axis=0) * scale


def sum_by_exchange(values, axes):
    copies = jnp.broadcast_to(values[None], (lax.axis_size(axes),) + values.shape)
    return jnp.sum(exchange(copies, axes), axis=0)


def own_share(values):
    count = lax.axis_size("z_hi")
    steps = [(h, (h + d) % count) for d in (1, 2, 3) for h in range(count)]
    place = {d: [(CORES * h, CORES * t) for h, t in steps if (t - h) % count == d] for d in (1, 3)}
    place[2] = [(CORES * h + 1, CORES * t + 1) for h, t in steps if (t - h) % count == 2]
    first = lax.ppermute(values, ("z_hi", "core"), place[1] + place[2])
    last = lax.ppermute(values, ("z_hi", "core"), place[3])
    own = jnp.where(lax.axis_index("core") == 0, values, jnp.zeros_like(values))
    return own + first + last


def in_thirds(values, shape):
    high = lax.reduce_precision(values, 8, 7)
    middle = lax.reduce_precision(values - high, 8, 7)
    low = values - high - middle
    rows = jnp.stack([high, middle, low, jnp.zeros_like(low)], axis=1).astype(BF16)
    return jnp.broadcast_to(rows.reshape(1, -1, shape[2]), (shape[0], 8, shape[2]))


def body(psi, dims, pattern, left_env, right_env):
    sectors = psi.shape[0]
    count = lax.axis_size(COL)
    core = lax.axis_index("core")
    swap = [(0, 1), (1, 0)]
    scale = 1.0 / jnp.sqrt(F32(right_env.shape[0] * count))
    coeff = jnp.broadcast_to(pattern.astype(F32)[None], (count // CORES,) + pattern.shape)
    coeff = lax.optimization_barrier(coeff)

    psi_m = masked(psi, dims)
    outgoing = combine(psi_m, coeff)
    left_mine = lax.dynamic_index_in_dim(left_env, core, 0, keepdims=False)
    left_sent = lax.dynamic_index_in_dim(left_env, 1 - core, 0, keepdims=False)
    left = jnp.concatenate([left_mine, lax.ppermute(left_sent, "core", swap)], axis=0)
    right = jnp.concatenate([right_env, lax.ppermute(right_env, "core", swap)], axis=0)
    left, right = lax.optimization_barrier((left, right))
    parts = exchange(product(exchange(outgoing, COL), left, right), COL)
    sigma = masked(reduced(parts, sectors, scale), dims)
    vector = psi_m.astype(F32)
    products = jnp.stack([jnp.sum(vector * sigma, axis=(0, 1)), jnp.sum(vector * vector, axis=(0, 1))])
    sums = sum_by_exchange(products, NEAR)
    outgoing = combine(sigma.astype(BF16), coeff)
    outgoing, sums = lax.optimization_barrier((outgoing, sums))
    share = own_share(sums)
    part = product(exchange(outgoing, COL), left, right)
    sent = jnp.concatenate([part, in_thirds(share, part.shape)], axis=1)
    parts = exchange(sent, COL)
    rows = part.shape[1]
    sums = jnp.sum(parts[:, rows:].astype(F32).reshape(count, 2, 4, -1), axis=(0, 2, 3))
    theta = sums[0] / sums[1]
    second = masked(reduced(parts[:, :rows], sectors, scale), dims) - theta * sigma
    return (sigma, second)


def solution(mesh):
    split = Mesh(mesh.devices.reshape(tuple(SPLIT.values())), tuple(SPLIT))
    return jax.shard_map(
        body,
        mesh=split,
        in_specs=(
            P(BLK, COL, None),
            P(BLK),
            P(BLK, None),
            P(BLK, COL, None, None),
            P(COL, None, None),
        ),
        out_specs=(P(BLK, COL, None), P(BLK, COL, None)),
        check_vma=False,
    )
```

```python
import jax
import jax.numpy as jnp
from jax import lax
from jax.sharding import Mesh, PartitionSpec as P

CORES = 2
LANES = 128
SPLIT = {"z_hi": 4, "x": 4, "y": 8, "z_lo": 3, "core": 2}
BLK = ("z_hi", "x", "y")
COL = ("z_lo", "core")
NEAR = ("x", "y", "core")
F32 = jnp.float32
BF16 = jnp.bfloat16


def exchange(blocks, axes):
    return lax.all_to_all(blocks, axes, 0, 0, tiled=True)


def masked(value, dims):
    _, rows, width = value.shape
    dims = lax.optimization_barrier(dims)[:, None, None]
    row = lax.broadcasted_iota(jnp.int32, value.shape, 1) + lax.axis_index(COL) * rows
    column = lax.broadcasted_iota(jnp.int32, value.shape, 2)
    return jnp.where((row < dims) & (column < dims), value, jnp.zeros_like(value))


def combine(vector, coeff):
    count = lax.axis_size(BLK)
    near = [(i, i ^ 1) for i in range(count)]
    across = [(i, i + 1 if i % 2 else i - 1) for i in range(1, count - 1)]
    other = lax.ppermute(vector, BLK, across)
    partner = lax.ppermute(vector, BLK, near)
    even = lax.rem(lax.axis_index(BLK), 2) == 0
    low, high = jnp.where(even, other, partner), jnp.where(even, partner, other)
    padded = jnp.concatenate([low, vector, high], axis=0).astype(F32)
    sectors, rows, width = vector.shape
    total = jnp.zeros(coeff.shape[:2] + (rows, width), F32)
    for offset in range(coeff.shape[2]):
        total = total + coeff[:, :, offset, None, None] * padded[None, offset : offset + sectors]
    return total.astype(BF16).reshape(-1, rows, width)


def product(z, left, right):
    count, rows, width = z.shape
    z = z.reshape(count * rows, width)
    temp = jnp.einsum("wab,bc->wac", left, z, preferred_element_type=F32).astype(BF16)
    part = jnp.einsum("wac,wdc->ad", temp, right, preferred_element_type=F32)
    return part.astype(BF16).reshape(count, rows, width)


def reduced(parts, sectors, scale):
    count, rows, width = parts.shape
    parts = parts.astype(F32).reshape(count // sectors, sectors, rows, width)
    return jnp.sum(parts, axis=0) * scale


def sum_by_exchange(values, axes):
    copies = jnp.broadcast_to(values[None], (lax.axis_size(axes),) + values.shape)
    return jnp.sum(exchange(copies, axes), axis=0)


def own_share(values):
    count = lax.axis_size("z_hi")
    steps = [(h, (h + d) % count) for d in (1, 2, 3) for h in range(count)]
    place = {d: [(CORES * h, CORES * t) for h, t in steps if (t - h) % count == d] for d in (1, 3)}
    place[2] = [(CORES * h + 1, CORES * t + 1) for h, t in steps if (t - h) % count == 2]
    first = lax.ppermute(values, ("z_hi", "core"), place[1] + place[2])
    last = lax.ppermute(values, ("z_hi", "core"), place[3])
    own = jnp.where(lax.axis_index("core") == 0, values, jnp.zeros_like(values))
    return own + first + last


def in_thirds(values, shape):
    high = lax.reduce_precision(values, 8, 7)
    middle = lax.reduce_precision(values - high, 8, 7)
    low = values - high - middle
    rows = jnp.stack([high, middle, low, jnp.zeros_like(low)], axis=1).astype(BF16)
    return jnp.broadcast_to(rows.reshape(1, -1, shape[2]), (shape[0], 8, shape[2]))


def body(psi, dims, pattern, left_env, right_env):
    sectors = psi.shape[0]
    count = lax.axis_size(COL)
    core = lax.axis_index("core")
    swap = [(0, 1), (1, 0)]
    scale = 1.0 / jnp.sqrt(F32(right_env.shape[0] * count))
    coeff = jnp.broadcast_to(pattern.astype(F32)[None], (count // CORES,) + pattern.shape)
    coeff = lax.optimization_barrier(coeff)

    psi_m = masked(psi, dims)
    outgoing = combine(psi_m, coeff)
    left_mine = lax.dynamic_index_in_dim(left_env, core, 0, keepdims=False)
    left_sent = lax.dynamic_index_in_dim(left_env, 1 - core, 0, keepdims=False)
    left = jnp.concatenate([left_mine, lax.ppermute(left_sent, "core", swap)], axis=0)
    right = jnp.concatenate([right_env, lax.ppermute(right_env, "core", swap)], axis=0)
    left, right = lax.optimization_barrier((left, right))
    parts = exchange(product(exchange(outgoing, COL), left, right), COL)
    sigma = masked(reduced(parts, sectors, scale), dims)
    vector = psi_m.astype(F32)
    products = jnp.stack([jnp.sum(vector * sigma, axis=(0, 1)), jnp.sum(vector * vector, axis=(0, 1))])
    sums = sum_by_exchange(products, NEAR)
    outgoing = combine(sigma.astype(BF16), coeff)
    outgoing, sums = lax.optimization_barrier((outgoing, sums))
    share = own_share(sums)
    part = product(exchange(outgoing, COL), left, right)
    sent = jnp.concatenate([part, in_thirds(share, part.shape)], axis=1)
    parts = exchange(sent, COL)
    rows = part.shape[1]
    sums = jnp.sum(parts[:, rows:].astype(F32).reshape(count, 2, 4, -1), axis=(0, 2))
    sums = jnp.broadcast_to(jnp.sum(sums, axis=1, keepdims=True), sums.shape)
    sums = lax.optimization_barrier(sums)
    theta = sums[0] / sums[1]
    second = masked(reduced(parts[:, :rows], sectors, scale), dims) - theta * sigma
    return (sigma, second)


def solution(mesh):
    split = Mesh(mesh.devices.reshape(tuple(SPLIT.values())), tuple(SPLIT))
    return jax.shard_map(
        body,
        mesh=split,
        in_specs=(
            P(BLK, COL, None),
            P(BLK),
            P(BLK, None),
            P(BLK, COL, None, None),
            P(COL, None, None),
        ),
        out_specs=(P(BLK, COL, None), P(BLK, COL, None)),
        check_vma=False,
    )
```

```python
import jax
import jax.numpy as jnp
from jax import lax
from jax.sharding import Mesh, PartitionSpec as P

CORES = 2
LANES = 128
SPLIT = {"z_hi": 4, "x": 4, "y": 8, "z_lo": 3, "core": 2}
BLK = ("z_hi", "x", "y")
COL = ("z_lo", "core")
NEAR = ("x", "y", "core")
F32 = jnp.float32
BF16 = jnp.bfloat16


def exchange(blocks, axes):
    return lax.all_to_all(blocks, axes, 0, 0, tiled=True)


def masked(value, dims):
    _, rows, width = value.shape
    dims = lax.optimization_barrier(dims)[:, None, None]
    row = lax.broadcasted_iota(jnp.int32, value.shape, 1) + lax.axis_index(COL) * rows
    column = lax.broadcasted_iota(jnp.int32, value.shape, 2)
    return jnp.where((row < dims) & (column < dims), value, jnp.zeros_like(value))


def combine(vector, coeff):
    count = lax.axis_size(BLK)
    near = [(i, i ^ 1) for i in range(count)]
    across = [(i, i + 1 if i % 2 else i - 1) for i in range(1, count - 1)]
    other = lax.ppermute(vector, BLK, across)
    partner = lax.ppermute(vector, BLK, near)
    even = lax.rem(lax.axis_index(BLK), 2) == 0
    low, high = jnp.where(even, other, partner), jnp.where(even, partner, other)
    padded = jnp.concatenate([low, vector, high], axis=0).astype(F32)
    sectors, rows, width = vector.shape
    total = jnp.zeros(coeff.shape[:2] + (rows, width), F32)
    for offset in range(coeff.shape[2]):
        total = total + coeff[:, :, offset, None, None] * padded[None, offset : offset + sectors]
    return total.astype(BF16).reshape(-1, rows, width)


def product(z, left, right):
    count, rows, width = z.shape
    z = z.reshape(count * rows, width)
    temp = jnp.einsum("wab,bc->wac", left, z, preferred_element_type=F32).astype(BF16)
    part = jnp.einsum("wac,wdc->ad", temp, right, preferred_element_type=F32)
    return part.astype(BF16).reshape(count, rows, width)


def reduced(parts, sectors, scale):
    count, rows, width = parts.shape
    parts = parts.astype(F32).reshape(count // sectors, sectors, rows, width)
    return jnp.sum(parts, axis=0) * scale


def sum_by_exchange(values, axes):
    copies = jnp.broadcast_to(values[None], (lax.axis_size(axes),) + values.shape)
    return jnp.sum(exchange(copies, axes), axis=0)


def own_share(values):
    count = lax.axis_size("z_hi")
    steps = [(h, (h + d) % count) for d in (1, 2, 3) for h in range(count)]
    place = {d: [(CORES * h, CORES * t) for h, t in steps if (t - h) % count == d] for d in (1, 3)}
    place[2] = [(CORES * h + 1, CORES * t + 1) for h, t in steps if (t - h) % count == 2]
    first = lax.ppermute(values, ("z_hi", "core"), place[1] + place[2])
    last = lax.ppermute(values, ("z_hi", "core"), place[3])
    own = jnp.where(lax.axis_index("core") == 0, values, jnp.zeros_like(values))
    return own, first, last


def in_thirds(values, shape):
    high = lax.reduce_precision(values, 8, 7)
    middle = lax.reduce_precision(values - high, 8, 7)
    low = values - high - middle
    rows = jnp.stack([high, middle, low, jnp.zeros_like(low)], axis=1).astype(BF16)
    return jnp.broadcast_to(rows.reshape(1, -1, shape[2]), (shape[0], 8, shape[2]))


def body(psi, dims, pattern, left_env, right_env):
    sectors = psi.shape[0]
    count = lax.axis_size(COL)
    core = lax.axis_index("core")
    swap = [(0, 1), (1, 0)]
    scale = 1.0 / jnp.sqrt(F32(right_env.shape[0] * count))
    coeff = jnp.broadcast_to(pattern.astype(F32)[None], (count // CORES,) + pattern.shape)
    coeff = lax.optimization_barrier(coeff)

    psi_m = masked(psi, dims)
    outgoing = combine(psi_m, coeff)
    left_mine = lax.dynamic_index_in_dim(left_env, core, 0, keepdims=False)
    left_sent = lax.dynamic_index_in_dim(left_env, 1 - core, 0, keepdims=False)
    left = jnp.concatenate([left_mine, lax.ppermute(left_sent, "core", swap)], axis=0)
    right = jnp.concatenate([right_env, lax.ppermute(right_env, "core", swap)], axis=0)
    left, right = lax.optimization_barrier((left, right))
    parts = exchange(product(exchange(outgoing, COL), left, right), COL)
    sigma = masked(reduced(parts, sectors, scale), dims)
    vector = psi_m.astype(F32)
    products = jnp.stack([jnp.sum(vector * sigma, axis=(0, 1)), jnp.sum(vector * vector, axis=(0, 1))])
    sums = sum_by_exchange(jnp.sum(products.reshape(2, -1, LANES), axis=1), NEAR)
    outgoing = combine(sigma.astype(BF16), coeff)
    outgoing, sums = lax.optimization_barrier((outgoing, sums))
    shares = own_share(sums)
    part = product(exchange(outgoing, COL), left, right)
    part, shares = lax.optimization_barrier((part, shares))
    share = jnp.pad(sum(shares), ((0, 0), (0, part.shape[2] - LANES)))
    sent = jnp.concatenate([part, in_thirds(share, part.shape)], axis=1)
    parts = exchange(sent, COL)
    rows = part.shape[1]
    sums = jnp.sum(parts[:, rows:].astype(F32).reshape(count, 2, 4, -1), axis=(0, 2))
    sums = jnp.broadcast_to(jnp.sum(sums, axis=1, keepdims=True), sums.shape)
    sums = lax.optimization_barrier(sums)
    theta = sums[0] / sums[1]
    second = masked(reduced(parts[:, :rows], sectors, scale), dims) - theta * sigma
    return (sigma, second)


def solution(mesh):
    split = Mesh(mesh.devices.reshape(tuple(SPLIT.values())), tuple(SPLIT))
    return jax.shard_map(
        body,
        mesh=split,
        in_specs=(
            P(BLK, COL, None),
            P(BLK),
            P(BLK, None),
            P(BLK, COL, None, None),
            P(COL, None, None),
        ),
        out_specs=(P(BLK, COL, None), P(BLK, COL, None)),
        check_vma=False,
    )
```

```python
import jax
import jax.numpy as jnp
from jax import lax
from jax.experimental import pallas as pl
from jax.experimental.pallas import tpu as pltpu
from jax.sharding import Mesh, PartitionSpec as P

CORES = 2
LANES = 128
SPLIT = {"z_hi": 4, "x": 4, "y": 8, "z_lo": 3, "core": 2}
BLK = ("z_hi", "x", "y")
COL = ("z_lo", "core")
NEAR = ("x", "y", "core")
F32 = jnp.float32
COST = 30_000_000_000
BF16 = jnp.bfloat16


def exchange(blocks, axes):
    return lax.all_to_all(blocks, axes, 0, 0, tiled=True)


def masked(value, dims):
    _, rows, width = value.shape
    dims = lax.optimization_barrier(dims)[:, None, None]
    row = lax.broadcasted_iota(jnp.int32, value.shape, 1) + lax.axis_index(COL) * rows
    column = lax.broadcasted_iota(jnp.int32, value.shape, 2)
    return jnp.where((row < dims) & (column < dims), value, jnp.zeros_like(value))


def neighbours(vector):
    count = lax.axis_size(BLK)
    near = [(i, i ^ 1) for i in range(count)]
    across = [(i, i + 1 if i % 2 else i - 1) for i in range(1, count - 1)]
    other = lax.ppermute(vector, BLK, across)
    partner = lax.ppermute(vector, BLK, near)
    even = lax.rem(lax.axis_index(BLK), 2) == 0
    return jnp.where(even, other, partner), jnp.where(even, partner, other)


def combine(low, vector, high, coeff):
    padded = jnp.concatenate([low, vector, high], axis=0).astype(F32)
    sectors, rows, width = vector.shape
    total = jnp.zeros(coeff.shape[:2] + (rows, width), F32)
    for offset in range(coeff.shape[2]):
        total = total + coeff[:, :, offset, None, None] * padded[None, offset : offset + sectors]
    return total.astype(BF16).reshape(-1, rows, width)


def product(z, left, right):
    count, rows, width = z.shape
    z = z.reshape(count * rows, width)
    temp = jnp.einsum("wab,bc->wac", left, z, preferred_element_type=F32).astype(BF16)
    part = jnp.einsum("wac,wdc->ad", temp, right, preferred_element_type=F32)
    return part.astype(BF16).reshape(count, rows, width)


def reduced(parts, sectors, scale):
    count, rows, width = parts.shape
    parts = parts.astype(F32).reshape(count // sectors, sectors, rows, width)
    return jnp.sum(parts, axis=0) * scale


def add_up(received):
    def kernel(received, total):
        total[...] = jnp.sum(received[...], axis=0)

    return pl.pallas_call(
        kernel,
        out_shape=jax.ShapeDtypeStruct(received.shape[1:], F32),
        in_specs=[pl.BlockSpec(memory_space=pltpu.VMEM)],
        out_specs=pl.BlockSpec(memory_space=pltpu.VMEM),
        cost_estimate=pl.CostEstimate(flops=COST, bytes_accessed=0, transcendentals=0),
    )(received)


def own_share(values):
    count = lax.axis_size("z_hi")
    steps = [(h, (h + d) % count) for d in (1, 2, 3) for h in range(count)]
    place = {d: [(CORES * h, CORES * t) for h, t in steps if (t - h) % count == d] for d in (1, 3)}
    place[2] = [(CORES * h + 1, CORES * t + 1) for h, t in steps if (t - h) % count == 2]
    first = lax.ppermute(values, ("z_hi", "core"), place[1] + place[2])
    last = lax.ppermute(values, ("z_hi", "core"), place[3])
    own = jnp.where(lax.axis_index("core") == 0, values, jnp.zeros_like(values))
    return own, first, last


def in_thirds(values, shape):
    high = lax.reduce_precision(values, 8, 7)
    middle = lax.reduce_precision(values - high, 8, 7)
    low = values - high - middle
    rows = jnp.stack([high, middle, low, jnp.zeros_like(low)], axis=1).astype(BF16)
    return jnp.broadcast_to(rows.reshape(1, -1, shape[2]), (shape[0], 8, shape[2]))


def body(psi, dims, pattern, left_env, right_env):
    sectors = psi.shape[0]
    count = lax.axis_size(COL)
    core = lax.axis_index("core")
    swap = [(0, 1), (1, 0)]
    scale = 1.0 / jnp.sqrt(F32(right_env.shape[0] * count))
    coeff = jnp.broadcast_to(pattern.astype(F32)[None], (count // CORES,) + pattern.shape)
    coeff = lax.optimization_barrier(coeff)

    psi_m = masked(psi, dims)
    low, high = neighbours(psi_m)
    outgoing = combine(low, psi_m, high, coeff)
    left_mine = lax.dynamic_index_in_dim(left_env, core, 0, keepdims=False)
    left_sent = lax.dynamic_index_in_dim(left_env, 1 - core, 0, keepdims=False)
    left = jnp.concatenate([left_mine, lax.ppermute(left_sent, "core", swap)], axis=0)
    right = jnp.concatenate([right_env, lax.ppermute(right_env, "core", swap)], axis=0)
    left, right = lax.optimization_barrier((left, right))
    parts = exchange(product(exchange(outgoing, COL), left, right), COL)
    sigma = masked(reduced(parts, sectors, scale), dims)
    vector = psi_m.astype(F32)
    products = jnp.stack([jnp.sum(vector * sigma, axis=(0, 1)), jnp.sum(vector * vector, axis=(0, 1))])
    products = jnp.sum(products.reshape(2, -1, LANES), axis=1)
    copies = jnp.broadcast_to(products[None], (lax.axis_size(NEAR),) + products.shape)
    sums = add_up(exchange(copies, NEAR))
    rounded = sigma.astype(BF16)
    low, high = neighbours(rounded)
    low, high, sums = lax.optimization_barrier((low, high, sums))
    outgoing = combine(low, rounded, high, coeff)
    shares = own_share(sums)
    part = product(exchange(outgoing, COL), left, right)
    part, shares = lax.optimization_barrier((part, shares))
    share = jnp.pad(sum(shares), ((0, 0), (0, part.shape[2] - LANES)))
    sent = jnp.concatenate([part, in_thirds(share, part.shape)], axis=1)
    parts = exchange(sent, COL)
    rows = part.shape[1]
    sums = jnp.sum(parts[:, rows:].astype(F32).reshape(count, 2, 4, -1), axis=(0, 2))
    sums = jnp.broadcast_to(jnp.sum(sums, axis=1, keepdims=True), sums.shape)
    sums = lax.optimization_barrier(sums)
    theta = sums[0] / sums[1]
    second = masked(reduced(parts[:, :rows], sectors, scale), dims) - theta * sigma
    return (sigma, second)


def solution(mesh):
    split = Mesh(mesh.devices.reshape(tuple(SPLIT.values())), tuple(SPLIT))
    return jax.shard_map(
        body,
        mesh=split,
        in_specs=(
            P(BLK, COL, None),
            P(BLK),
            P(BLK, None),
            P(BLK, COL, None, None),
            P(COL, None, None),
        ),
        out_specs=(P(BLK, COL, None), P(BLK, COL, None)),
        check_vma=False,
    )
```

```python
import jax
import jax.numpy as jnp
from jax import lax
from jax.experimental import pallas as pl
from jax.experimental.pallas import tpu as pltpu
from jax.sharding import Mesh, PartitionSpec as P

CORES = 2
LANES = 128
SPLIT = {"z_hi": 4, "x": 4, "y": 8, "z_lo": 3, "core": 2}
BLK = ("z_hi", "x", "y")
COL = ("z_lo", "core")
NEAR = ("x", "y", "core")
F32 = jnp.float32
COST = 30_000_000_000
BF16 = jnp.bfloat16


def exchange(blocks, axes):
    return lax.all_to_all(blocks, axes, 0, 0, tiled=True)


def masked(value, dims):
    _, rows, width = value.shape
    dims = lax.optimization_barrier(dims)[:, None, None]
    row = lax.broadcasted_iota(jnp.int32, value.shape, 1) + lax.axis_index(COL) * rows
    column = lax.broadcasted_iota(jnp.int32, value.shape, 2)
    return jnp.where((row < dims) & (column < dims), value, jnp.zeros_like(value))


def neighbours(vector):
    count = lax.axis_size(BLK)
    near = [(i, i ^ 1) for i in range(count)]
    across = [(i, i + 1 if i % 2 else i - 1) for i in range(1, count - 1)]
    other = lax.ppermute(vector, BLK, across)
    partner = lax.ppermute(vector, BLK, near)
    return other, partner


def combine(other, vector, partner, coeff):
    even = lax.rem(lax.axis_index(BLK), 2) == 0
    low, high = jnp.where(even, other, partner), jnp.where(even, partner, other)
    padded = jnp.concatenate([low, vector, high], axis=0).astype(F32)
    sectors, rows, width = vector.shape
    total = jnp.zeros(coeff.shape[:2] + (rows, width), F32)
    for offset in range(coeff.shape[2]):
        total = total + coeff[:, :, offset, None, None] * padded[None, offset : offset + sectors]
    return total.astype(BF16).reshape(-1, rows, width)


def product(z, left, right):
    count, rows, width = z.shape
    z = z.reshape(count * rows, width)
    temp = jnp.einsum("wab,bc->wac", left, z, preferred_element_type=F32).astype(BF16)
    part = jnp.einsum("wac,wdc->ad", temp, right, preferred_element_type=F32)
    return part.astype(BF16).reshape(count, rows, width)


def reduced(parts, sectors, scale):
    count, rows, width = parts.shape
    parts = parts.astype(F32).reshape(count // sectors, sectors, rows, width)
    return jnp.sum(parts, axis=0) * scale


def add_up(received):
    def kernel(received, total):
        total[...] = jnp.sum(received[...], axis=0)

    return pl.pallas_call(
        kernel,
        out_shape=jax.ShapeDtypeStruct(received.shape[1:], F32),
        in_specs=[pl.BlockSpec(memory_space=pltpu.VMEM)],
        out_specs=pl.BlockSpec(memory_space=pltpu.VMEM),
        cost_estimate=pl.CostEstimate(flops=COST, bytes_accessed=0, transcendentals=0),
    )(received)


def own_share(values):
    count = lax.axis_size("z_hi")
    steps = [(h, (h + d) % count) for d in (1, 2, 3) for h in range(count)]
    place = {d: [(CORES * h, CORES * t) for h, t in steps if (t - h) % count == d] for d in (1, 3)}
    place[2] = [(CORES * h + 1, CORES * t + 1) for h, t in steps if (t - h) % count == 2]
    first = lax.ppermute(values, ("z_hi", "core"), place[1] + place[2])
    last = lax.ppermute(values, ("z_hi", "core"), place[3])
    own = jnp.where(lax.axis_index("core") == 0, values, jnp.zeros_like(values))
    return own, first, last


def in_thirds(values, shape):
    high = lax.reduce_precision(values, 8, 7)
    middle = lax.reduce_precision(values - high, 8, 7)
    low = values - high - middle
    rows = jnp.stack([high, middle, low, jnp.zeros_like(low)], axis=1).astype(BF16)
    return jnp.broadcast_to(rows.reshape(1, -1, shape[2]), (shape[0], 8, shape[2]))


def body(psi, dims, pattern, left_env, right_env):
    sectors = psi.shape[0]
    count = lax.axis_size(COL)
    core = lax.axis_index("core")
    swap = [(0, 1), (1, 0)]
    scale = 1.0 / jnp.sqrt(F32(right_env.shape[0] * count))
    coeff = jnp.broadcast_to(pattern.astype(F32)[None], (count // CORES,) + pattern.shape)
    coeff = lax.optimization_barrier(coeff)

    psi_m = masked(psi, dims)
    other, partner = neighbours(psi_m)
    outgoing = combine(other, psi_m, partner, coeff)
    left_mine = lax.dynamic_index_in_dim(left_env, core, 0, keepdims=False)
    left_sent = lax.dynamic_index_in_dim(left_env, 1 - core, 0, keepdims=False)
    left = jnp.concatenate([left_mine, lax.ppermute(left_sent, "core", swap)], axis=0)
    right = jnp.concatenate([right_env, lax.ppermute(right_env, "core", swap)], axis=0)
    left, right = lax.optimization_barrier((left, right))
    parts = exchange(product(exchange(outgoing, COL), left, right), COL)
    sigma = masked(reduced(parts, sectors, scale), dims)
    vector = psi_m.astype(F32)
    products = jnp.stack([jnp.sum(vector * sigma, axis=(0, 1)), jnp.sum(vector * vector, axis=(0, 1))])
    products = jnp.sum(products.reshape(2, -1, LANES), axis=1)
    copies = jnp.broadcast_to(products[None], (lax.axis_size(NEAR),) + products.shape)
    sums = add_up(exchange(copies, NEAR))
    rounded = sigma.astype(BF16)
    other, partner = neighbours(rounded)
    other, partner, sums = lax.optimization_barrier((other, partner, sums))
    outgoing = combine(other, rounded, partner, coeff)
    shares = own_share(sums)
    part = product(exchange(outgoing, COL), left, right)
    part, shares = lax.optimization_barrier((part, shares))
    share = jnp.pad(sum(shares), ((0, 0), (0, part.shape[2] - LANES)))
    sent = jnp.concatenate([part, in_thirds(share, part.shape)], axis=1)
    parts = exchange(sent, COL)
    rows = part.shape[1]
    sums = jnp.sum(parts[:, rows:].astype(F32).reshape(count, 2, 4, -1), axis=(0, 2))
    sums = jnp.broadcast_to(jnp.sum(sums, axis=1, keepdims=True), sums.shape)
    sums = lax.optimization_barrier(sums)
    theta = sums[0] / sums[1]
    second = masked(reduced(parts[:, :rows], sectors, scale), dims) - theta * sigma
    return (sigma, second)


def solution(mesh):
    split = Mesh(mesh.devices.reshape(tuple(SPLIT.values())), tuple(SPLIT))
    return jax.shard_map(
        body,
        mesh=split,
        in_specs=(
            P(BLK, COL, None),
            P(BLK),
            P(BLK, None),
            P(BLK, COL, None, None),
            P(COL, None, None),
        ),
        out_specs=(P(BLK, COL, None), P(BLK, COL, None)),
        check_vma=False,
    )
```

```python
import jax
import jax.numpy as jnp
from jax import lax
from jax.experimental import pallas as pl
from jax.experimental.pallas import tpu as pltpu
from jax.sharding import Mesh, PartitionSpec as P

CORES = 2
LANES = 128
SPLIT = {"z_hi": 4, "x": 4, "y": 8, "z_lo": 3, "core": 2}
BLK = ("z_hi", "x", "y")
COL = ("z_lo", "core")
NEAR = ("x", "y", "core")
F32 = jnp.float32
COST = 30_000_000_000
BF16 = jnp.bfloat16


def exchange(blocks, axes):
    return lax.all_to_all(blocks, axes, 0, 0, tiled=True)


def masked(value, dims):
    _, rows, width = value.shape
    dims = lax.optimization_barrier(dims)[:, None, None]
    row = lax.broadcasted_iota(jnp.int32, value.shape, 1) + lax.axis_index(COL) * rows
    column = lax.broadcasted_iota(jnp.int32, value.shape, 2)
    return jnp.where((row < dims) & (column < dims), value, jnp.zeros_like(value))


def neighbours(vector):
    count = lax.axis_size(BLK)
    near = [(i, i ^ 1) for i in range(count)]
    across = [(i, i + 1 if i % 2 else i - 1) for i in range(1, count - 1)]
    other = lax.ppermute(vector, BLK, across)
    partner = lax.ppermute(vector, BLK, near)
    return other, partner


def combine(other, vector, partner, coeff):
    even = lax.rem(lax.axis_index(BLK), 2) == 0
    low, high = jnp.where(even, other, partner), jnp.where(even, partner, other)
    padded = jnp.concatenate([low, vector, high], axis=0).astype(F32)
    sectors, rows, width = vector.shape
    total = jnp.zeros(coeff.shape[:2] + (rows, width), F32)
    for offset in range(coeff.shape[2]):
        total = total + coeff[:, :, offset, None, None] * padded[None, offset : offset + sectors]
    return total.astype(BF16).reshape(-1, rows, width)


def product(z, left, right):
    count, rows, width = z.shape
    z = z.reshape(count * rows, width)
    temp = jnp.einsum("wab,bc->wac", left, z, preferred_element_type=F32).astype(BF16)
    part = jnp.einsum("wac,wdc->ad", temp, right, preferred_element_type=F32)
    return part.astype(BF16).reshape(count, rows, width)


def reduced(parts, sectors, scale):
    count, rows, width = parts.shape
    parts = parts.astype(F32).reshape(count // sectors, sectors, rows, width)
    return jnp.sum(parts, axis=0) * scale


def add_up(received):
    def kernel(received, total):
        total[...] = jnp.sum(received[...], axis=0)

    return pl.pallas_call(
        kernel,
        out_shape=jax.ShapeDtypeStruct(received.shape[1:], F32),
        in_specs=[pl.BlockSpec(memory_space=pltpu.VMEM)],
        out_specs=pl.BlockSpec(memory_space=pltpu.VMEM),
        cost_estimate=pl.CostEstimate(flops=COST, bytes_accessed=0, transcendentals=0),
    )(received)


def own_share(values):
    planes = lax.axis_size("z_hi")
    places = lax.axis_size(("x", "y"))
    edge = lax.axis_size("y") - 1
    source = {0: edge, edge: places - 1, places - 1: 0}

    def pairs(distance, core):
        return [
            (
                (plane * places + source.get(place, place)) * CORES + core,
                ((plane + distance) % planes * places + place) * CORES + core,
            )
            for plane in range(planes)
            for place in range(places)
        ]

    axes = ("z_hi", "x", "y", "core")
    first = lax.ppermute(values, axes, pairs(1, 0) + pairs(2, 1))
    last = lax.ppermute(values, axes, pairs(3, 0))
    own = jnp.where(lax.axis_index("core") == 0, values, jnp.zeros_like(values))
    return own, first, last


def in_thirds(values, shape):
    high = lax.reduce_precision(values, 8, 7)
    middle = lax.reduce_precision(values - high, 8, 7)
    low = values - high - middle
    rows = jnp.stack([high, middle, low, jnp.zeros_like(low)], axis=1).astype(BF16)
    return jnp.broadcast_to(rows.reshape(1, -1, shape[2]), (shape[0], 8, shape[2]))


def body(psi, dims, pattern, left_env, right_env):
    sectors = psi.shape[0]
    count = lax.axis_size(COL)
    core = lax.axis_index("core")
    swap = [(0, 1), (1, 0)]
    scale = 1.0 / jnp.sqrt(F32(right_env.shape[0] * count))
    coeff = jnp.broadcast_to(pattern.astype(F32)[None], (count // CORES,) + pattern.shape)
    coeff = lax.optimization_barrier(coeff)

    psi_m = masked(psi, dims)
    other, partner = neighbours(psi_m)
    outgoing = combine(other, psi_m, partner, coeff)
    left_mine = lax.dynamic_index_in_dim(left_env, core, 0, keepdims=False)
    left_sent = lax.dynamic_index_in_dim(left_env, 1 - core, 0, keepdims=False)
    left = jnp.concatenate([left_mine, lax.ppermute(left_sent, "core", swap)], axis=0)
    right = jnp.concatenate([right_env, lax.ppermute(right_env, "core", swap)], axis=0)
    left, right = lax.optimization_barrier((left, right))
    parts = exchange(product(exchange(outgoing, COL), left, right), COL)
    sigma = masked(reduced(parts, sectors, scale), dims)
    vector = psi_m.astype(F32)
    products = jnp.stack([jnp.sum(vector * sigma, axis=(0, 1)), jnp.sum(vector * vector, axis=(0, 1))])
    products = jnp.sum(products.reshape(2, -1, LANES), axis=1)
    copies = jnp.broadcast_to(products[None], (lax.axis_size(NEAR),) + products.shape)
    sums = add_up(exchange(copies, NEAR))
    rounded = sigma.astype(BF16)
    other, partner = neighbours(rounded)
    other, partner, sums = lax.optimization_barrier((other, partner, sums))
    outgoing = combine(other, rounded, partner, coeff)
    shares = own_share(sums)
    part = product(exchange(outgoing, COL), left, right)
    part, shares = lax.optimization_barrier((part, shares))
    share = jnp.pad(sum(shares), ((0, 0), (0, part.shape[2] - LANES)))
    sent = jnp.concatenate([part, in_thirds(share, part.shape)], axis=1)
    parts = exchange(sent, COL)
    rows = part.shape[1]
    sums = jnp.sum(parts[:, rows:].astype(F32).reshape(count, 2, 4, -1), axis=(0, 2))
    sums = jnp.broadcast_to(jnp.sum(sums, axis=1, keepdims=True), sums.shape)
    sums = lax.optimization_barrier(sums)
    theta = sums[0] / sums[1]
    second = masked(reduced(parts[:, :rows], sectors, scale), dims) - theta * sigma
    return (sigma, second)


def solution(mesh):
    split = Mesh(mesh.devices.reshape(tuple(SPLIT.values())), tuple(SPLIT))
    return jax.shard_map(
        body,
        mesh=split,
        in_specs=(
            P(BLK, COL, None),
            P(BLK),
            P(BLK, None),
            P(BLK, COL, None, None),
            P(COL, None, None),
        ),
        out_specs=(P(BLK, COL, None), P(BLK, COL, None)),
        check_vma=False,
    )
```

```python
import jax
import jax.numpy as jnp
from jax import lax
from jax.experimental import pallas as pl
from jax.experimental.pallas import tpu as pltpu
from jax.sharding import Mesh, PartitionSpec as P

CORES = 2
LANES = 128
SPLIT = {"z_hi": 4, "x": 4, "y": 8, "z_lo": 3, "core": 2}
BLK = ("z_hi", "x", "y")
COL = ("z_lo", "core")
NEAR = ("x", "y", "core")
F32 = jnp.float32
COST = 30_000_000_000
BF16 = jnp.bfloat16


def exchange(blocks, axes):
    return lax.all_to_all(blocks, axes, 0, 0, tiled=True)


def masked(value, dims):
    _, rows, width = value.shape
    dims = lax.optimization_barrier(dims)[:, None, None]
    row = lax.broadcasted_iota(jnp.int32, value.shape, 1) + lax.axis_index(COL) * rows
    column = lax.broadcasted_iota(jnp.int32, value.shape, 2)
    return jnp.where((row < dims) & (column < dims), value, jnp.zeros_like(value))


def neighbours(vector):
    count = lax.axis_size(BLK)
    near = [(i, i ^ 1) for i in range(count)]
    across = [(i, i + 1 if i % 2 else i - 1) for i in range(1, count - 1)]
    other = lax.ppermute(vector, BLK, across)
    partner = lax.ppermute(vector, BLK, near)
    return other, partner


def combine(other, vector, partner, coeff):
    even = lax.rem(lax.axis_index(BLK), 2) == 0
    low, high = jnp.where(even, other, partner), jnp.where(even, partner, other)
    padded = jnp.concatenate([low, vector, high], axis=0).astype(F32)
    sectors, rows, width = vector.shape
    total = jnp.zeros(coeff.shape[:2] + (rows, width), F32)
    for offset in range(coeff.shape[2]):
        total = total + coeff[:, :, offset, None, None] * padded[None, offset : offset + sectors]
    return total.astype(BF16).reshape(-1, rows, width)


def product(z, left, right):
    count, rows, width = z.shape
    z = z.reshape(count * rows, width)
    temp = jnp.einsum("wab,bc->wac", left, z, preferred_element_type=F32).astype(BF16)
    part = jnp.einsum("wac,wdc->ad", temp, right, preferred_element_type=F32)
    return part.astype(BF16).reshape(count, rows, width)


def reduced(parts, sectors, scale):
    count, rows, width = parts.shape
    parts = parts.astype(F32).reshape(count // sectors, sectors, rows, width)
    return jnp.sum(parts, axis=0) * scale


def add_up(received):
    def kernel(received, total):
        total[...] = jnp.sum(received[...], axis=0)

    return pl.pallas_call(
        kernel,
        out_shape=jax.ShapeDtypeStruct(received.shape[1:], F32),
        in_specs=[pl.BlockSpec(memory_space=pltpu.VMEM)],
        out_specs=pl.BlockSpec(memory_space=pltpu.VMEM),
        cost_estimate=pl.CostEstimate(flops=COST, bytes_accessed=0, transcendentals=0),
    )(received)


def own_share(values):
    count = lax.axis_size("z_hi")
    steps = [(h, (h + d) % count) for d in (1, 2, 3) for h in range(count)]
    place = {d: [(CORES * h, CORES * t) for h, t in steps if (t - h) % count == d] for d in (1, 3)}
    place[2] = [(CORES * h + 1, CORES * t + 1) for h, t in steps if (t - h) % count == 2]
    first = lax.ppermute(values, ("z_hi", "core"), place[1] + place[2])
    last = lax.ppermute(values, ("z_hi", "core"), place[3])
    own = jnp.where(lax.axis_index("core") == 0, values, jnp.zeros_like(values))
    return own, first, last


def in_thirds(values, shape):
    high = lax.reduce_precision(values, 8, 7)
    middle = lax.reduce_precision(values - high, 8, 7)
    low = values - high - middle
    rows = jnp.stack([high, middle, low, jnp.zeros_like(low)], axis=1).astype(BF16)
    return jnp.broadcast_to(rows.reshape(1, -1, shape[2]), (shape[0], 8, shape[2]))


def body(psi, dims, pattern, left_env, right_env):
    sectors = psi.shape[0]
    count = lax.axis_size(COL)
    core = lax.axis_index("core")
    swap = [(0, 1), (1, 0)]
    scale = 1.0 / jnp.sqrt(F32(right_env.shape[0] * count))
    coeff = jnp.broadcast_to(pattern.astype(F32)[None], (count // CORES,) + pattern.shape)
    coeff = lax.optimization_barrier(coeff)

    psi_m = masked(psi, dims)
    other, partner = neighbours(psi_m)
    outgoing = combine(other, psi_m, partner, coeff)
    left_mine = lax.dynamic_index_in_dim(left_env, core, 0, keepdims=False)
    left_sent = lax.dynamic_index_in_dim(left_env, 1 - core, 0, keepdims=False)
    left = jnp.concatenate([left_mine, lax.ppermute(left_sent, "core", swap)], axis=0)
    right = jnp.concatenate([right_env, lax.ppermute(right_env, "core", swap)], axis=0)
    left, right = lax.optimization_barrier((left, right))
    parts = exchange(product(exchange(outgoing, COL), left, right), COL)
    sigma = masked(reduced(parts, sectors, scale), dims)
    vector = psi_m.astype(F32)
    products = jnp.stack([jnp.sum(vector * sigma, axis=(0, 1)), jnp.sum(vector * vector, axis=(0, 1))])
    products = jnp.sum(products.reshape(2, -1, LANES), axis=1)
    copies = jnp.broadcast_to(products[None], (lax.axis_size(NEAR),) + products.shape)
    sums = add_up(exchange(copies, NEAR))
    rounded = sigma.astype(BF16)
    other, partner = neighbours(rounded)
    partner, other, sums = lax.optimization_barrier((partner, other, sums))
    outgoing = combine(other, rounded, partner, coeff)
    shares = own_share(sums)
    part = product(exchange(outgoing, COL), left, right)
    part, shares = lax.optimization_barrier((part, shares))
    share = jnp.pad(sum(shares), ((0, 0), (0, part.shape[2] - LANES)))
    sent = jnp.concatenate([part, in_thirds(share, part.shape)], axis=1)
    parts = exchange(sent, COL)
    rows = part.shape[1]
    sums = jnp.sum(parts[:, rows:].astype(F32).reshape(count, 2, 4, -1), axis=(0, 2))
    sums = jnp.broadcast_to(jnp.sum(sums, axis=1, keepdims=True), sums.shape)
    sums = lax.optimization_barrier(sums)
    theta = sums[0] / sums[1]
    second = masked(reduced(parts[:, :rows], sectors, scale), dims) - theta * sigma
    return (sigma, second)


def solution(mesh):
    split = Mesh(mesh.devices.reshape(tuple(SPLIT.values())), tuple(SPLIT))
    return jax.shard_map(
        body,
        mesh=split,
        in_specs=(
            P(BLK, COL, None),
            P(BLK),
            P(BLK, None),
            P(BLK, COL, None, None),
            P(COL, None, None),
        ),
        out_specs=(P(BLK, COL, None), P(BLK, COL, None)),
        check_vma=False,
    )
```
